32 devices in a mesh: grp: 2 (over core), dev: 16 (over z, y, x).
Axes of the slice: x: 2, y: 2, z: 4, core: 2. Of those that a mesh axis runs over, the one named last changes fastest.
Arguments:
- images: bfloat16 [16384, 64, 128], P(('grp', 'dev')), may hold values from -6 to 6
- test_maps: bfloat16 [64, 128, 32], replicated, may hold values from -6 to 6
- counts: int32 [64], replicated, may hold values from 24 to 64, as said below
Outputs:
- projected: bfloat16 [16384, 64, 32], P(('grp', 'dev'))
The draws below stay inside these ranges and needn't reach their ends.
Inputs may be any that keep to these rules, and one draw needn't show every extreme that they name: `counts`: block 0 has 64 radial functions and block 63 has 24.
All inputs are finite; a program needn't handle non-finite values.
Results may differ from the reference program's by a relative error of at most 0.0049.
Values may be sent and summed in bfloat16 or wider, within the bound.
A program may use at most 64 MiB of HBM per device.

```python
import jax
import jax.numpy as jnp
from jax import lax

FREQ = 64
R = 64
RANK = 32
RAD_MIN = 24
IMAGES = 16384


def draw_counts(key, part):
    values = jax.random.randint(jax.random.fold_in(key, 7), (FREQ,), RAD_MIN, R + 1)
    values = values.at[0].set(R).at[FREQ - 1].set(RAD_MIN)
    return values.astype(jnp.int32)


def raised(array, key, source, target, parts, factor):
    def block_of(dim):
        return (jnp.arange(array.shape[dim]) // (array.shape[dim] // parts)).reshape((-1,) + (1,) * (array.ndim - 1 - dim))

    one_side = jax.random.permutation(key, parts)[block_of(target)]
    far = (block_of(target) + parts // 2) % parts
    return jnp.where((block_of(source) == one_side) | (block_of(source) == far), factor * array, array)


def block_levels(stream_key, extent, cuts, low, largest):
    def one(dim, blocks):
        heights = jax.random.uniform(jax.random.fold_in(jax.random.fold_in(stream_key, 6), dim), (blocks,), jnp.float32, low / len(cuts), largest / len(cuts))
        return jnp.repeat(jnp.exp(heights), extent[dim] // blocks).reshape((-1,) + (1,) * (len(extent) - dim - 1))

    factor_of = one(*cuts[0])
    for cut in cuts[1:]:
        factor_of = factor_of * one(*cut)
    return factor_of


def noise(rng, extent, scale, bound, split=(), dtype=jnp.bfloat16):
    entries = scale * jax.random.normal(rng, extent, jnp.float32)
    if split:
        entries = entries * block_levels(rng, extent, split, -0.22, 0.18)
    return jnp.clip(entries, -bound, bound).astype(dtype)


def gaussian_with(stream_key, shape, width, most, cuts, heavy, held_as=jnp.bfloat16):
    drawn = width * jax.random.normal(stream_key, shape, jnp.float32)
    if cuts:
        drawn = drawn * block_levels(stream_key, shape, cuts, -0.22, 0.18)
    return jnp.clip(raised(drawn, jax.random.fold_in(stream_key, 3), *heavy), -most, most).astype(held_as)


def setup_inputs(seed: int = 0) -> dict:
    keys = jax.random.split(jax.random.key(seed), 4)
    images = gaussian_with(keys[0], (IMAGES, FREQ, 2 * R), 1.0, 6.0, ((0, 32),), (0, 1, 32, 2.75))
    test_maps = noise(keys[1], (FREQ, 2 * R, RANK), 1.0, 6.0)
    counts = draw_counts(jax.random.fold_in(keys[3], 71), 0)
    return {"images": images, "test_maps": test_maps, "counts": counts}


def orthonormal(summed):
    gram_matrix = jnp.einsum('krs,krt->kst', summed, summed, precision=lax.Precision.HIGHEST)
    factor = jnp.linalg.cholesky(gram_matrix)
    solved = lax.linalg.triangular_solve(factor, summed, left_side=False, lower=True, transpose_a=True)
    return solved.astype(jnp.bfloat16)

def reference(images, test_maps, counts):
    columns = images.shape[2]
    radial = columns // 2
    position = lax.broadcasted_iota(jnp.int32, (images.shape[1], columns), 1) % radial
    valid_mask = (position < counts[:, None]).astype(jnp.bfloat16)
    masked = images * valid_mask[None]
    masked_wide = masked.astype(jnp.float32)
    sketch = jnp.einsum('ikr,krs->iks', masked_wide, test_maps.astype(jnp.float32)).astype(jnp.bfloat16)
    summed = jnp.einsum('ikr,iks->krs', masked_wide, sketch.astype(jnp.float32))
    basis_all = orthonormal(summed)
    projected = jnp.einsum('ikr,krs->iks', masked_wide, basis_all.astype(jnp.float32))
    return projected.astype(jnp.bfloat16)
```

```python
import functools

import jax
import jax.numpy as jnp
from jax import lax
from jax.experimental import pallas as pl
from jax.experimental.pallas import tpu as pltpu
from jax.sharding import PartitionSpec as P

MESH = pl.DeviceIdType.MESH


def orthonormal(summed):
    gram_matrix = jnp.einsum("krs,krt->kst", summed, summed, precision=lax.Precision.HIGHEST)
    factor = jnp.linalg.cholesky(gram_matrix)
    solved = lax.linalg.triangular_solve(
        factor, summed, left_side=False, lower=True, transpose_a=True
    )
    return solved.astype(jnp.bfloat16)


def basis_kernel(groups, devs, part_ref, out_ref, pair, half, slots, work, gath,
                 pair_send, pair_recv, sum_send, sum_recv, all_send, all_recv,
                 share_send, share_recv):
    me_g, me_d = lax.axis_index("grp"), lax.axis_index("dev")
    blocks, rank, columns = part_ref.shape
    per_group = blocks // groups
    own = per_group // devs

    barrier = pltpu.get_barrier_semaphore()
    for step in range(1, groups):
        pl.semaphore_signal(barrier, inc=1, device_id=((me_g + step) % groups, me_d), device_id_type=MESH)

    @pl.loop(1, devs)
    def _(step):
        pl.semaphore_signal(barrier, inc=1, device_id=(me_g, (me_d + step) % devs), device_id_type=MESH)

    pl.semaphore_wait(barrier, groups - 1 + devs - 1)

    pair_copies = []
    for step in range(1, groups):
        peer = (me_g + step) % groups
        copy = pltpu.make_async_remote_copy(
            src_ref=part_ref.at[pl.ds(peer * per_group, per_group)],
            dst_ref=pair.at[step - 1],
            send_sem=pair_send.at[step - 1],
            recv_sem=pair_recv.at[step - 1],
            device_id=(peer, me_d),
            device_id_type=MESH,
        )
        copy.start()
        pair_copies.append(copy)
    for copy in pair_copies:
        copy.wait()

    @pl.loop(0, per_group)
    def _(b):
        value = part_ref[me_g * per_group + b]
        for step in range(1, groups):
            value += pair[step - 1, b]
        half[b] = value

    def to_owner(step):
        target = (me_d + step) % devs
        return pltpu.make_async_remote_copy(
            src_ref=half.at[pl.ds(target * own, own)],
            dst_ref=slots.at[step],
            send_sem=sum_send.at[step],
            recv_sem=sum_recv.at[step],
            device_id=(me_g, target),
            device_id_type=MESH,
        )

    @pl.loop(1, devs)
    def _(step):
        to_owner(step).start()

    work[...] = half[pl.ds(me_d * own, own)]

    @pl.loop(1, devs)
    def _(step):
        to_owner(step).wait()
        work[...] += slots[step]

    position = lax.broadcasted_iota(jnp.int32, (own, rank, columns), 1)

    @pl.loop(0, rank)
    def _(j):
        rows = work[...]
        row = work[:, pl.ds(j, 1), :]
        along = jnp.sum(rows * row, axis=2, keepdims=True)
        scale = lax.rsqrt(jnp.sum(row * row, axis=2, keepdims=True))
        unit = row * scale
        later = rows - (along * scale) * unit
        work[...] = jnp.where(position > j, later, jnp.where(position == j, jnp.broadcast_to(unit, rows.shape), rows))

    mine = me_g * per_group + me_d * own
    gath[pl.ds(mine, own)] = work[...].astype(gath.dtype)

    def to_all(step):
        return pltpu.make_async_remote_copy(
            src_ref=gath.at[pl.ds(mine, own)],
            dst_ref=gath.at[pl.ds(mine, own)],
            send_sem=all_send.at[step],
            recv_sem=all_recv.at[step],
            device_id=(me_g, (me_d + step) % devs),
            device_id_type=MESH,
        )

    @pl.loop(1, devs)
    def _(step):
        to_all(step).start()

    @pl.loop(1, devs)
    def _(step):
        to_all(step).wait()

    share_copies = []
    for step in range(1, groups):
        part = gath.at[pl.ds(me_g * per_group, per_group)]
        copy = pltpu.make_async_remote_copy(
            src_ref=part,
            dst_ref=part,
            send_sem=share_send.at[step - 1],
            recv_sem=share_recv.at[step - 1],
            device_id=((me_g + step) % groups, me_d),
            device_id_type=MESH,
        )
        copy.start()
        share_copies.append(copy)
    for copy in share_copies:
        copy.wait()

    @pl.loop(0, blocks)
    def _(b):
        out_ref[b] = gath[b]


def all_bases(groups, devs, partial):
    blocks, rank, columns = partial.shape
    per_group = blocks // groups
    own = per_group // devs
    dma = pltpu.SemaphoreType.DMA
    return pl.pallas_call(
        functools.partial(basis_kernel, groups, devs),
        out_shape=jax.ShapeDtypeStruct(partial.shape, jnp.bfloat16),
        in_specs=[pl.BlockSpec(memory_space=pltpu.VMEM)],
        out_specs=pl.BlockSpec(memory_space=pltpu.VMEM),
        scratch_shapes=[
            pltpu.VMEM((groups - 1, per_group, rank, columns), jnp.float32),
            pltpu.VMEM((per_group, rank, columns), jnp.float32),
            pltpu.VMEM((devs, own, rank, columns), jnp.float32),
            pltpu.VMEM((own, rank, columns), jnp.float32),
            pltpu.VMEM(partial.shape, jnp.bfloat16),
            dma((groups - 1,)),
            dma((groups - 1,)),
            dma((devs,)),
            dma((devs,)),
            dma((devs,)),
            dma((devs,)),
            dma((groups - 1,)),
            dma((groups - 1,)),
        ],
        compiler_params=pltpu.CompilerParams(
            collective_id=0, has_side_effects=True, vmem_limit_bytes=24 * 1024 * 1024
        ),
    )(partial)


def body(groups, devs, images, test_maps, counts):
    blocks, columns = images.shape[1:]
    radial = columns // 2
    position = lax.broadcasted_iota(jnp.int32, (blocks, columns), 1) % radial
    valid = position < counts[:, None]
    maps = jnp.where(valid[:, :, None], test_maps, jnp.zeros_like(test_maps))
    sketch = jnp.einsum(
        "ikr,krs->iks", images, maps, preferred_element_type=jnp.float32
    ).astype(jnp.bfloat16)
    if groups > 1 and devs > 1 and blocks % (groups * devs) == 0:
        partial = jnp.einsum("ikr,iks->ksr", images, sketch, preferred_element_type=jnp.float32)
        partial = jnp.where(valid[:, None, :], partial, 0.0)
        basis_all = all_bases(groups, devs, partial)
        projected = jnp.einsum("ikr,ksr->iks", images, basis_all, preferred_element_type=jnp.float32)
    else:
        partial = jnp.einsum("ikr,iks->krs", images, sketch, preferred_element_type=jnp.float32)
        partial = jnp.where(valid[:, :, None], partial, 0.0)
        totals = lax.psum(partial, "grp")
        owned = lax.psum_scatter(totals, "dev", scatter_dimension=0, tiled=True)
        basis_all = lax.all_gather(orthonormal(owned), "dev", axis=0, tiled=True)
        projected = jnp.einsum("ikr,krs->iks", images, basis_all, preferred_element_type=jnp.float32)
    return projected.astype(jnp.bfloat16)


def solution(mesh):
    in_specs = (P(("grp", "dev"), None, None), P(), P())
    out_specs = P(("grp", "dev"), None, None)
    part = functools.partial(body, mesh.shape["grp"], mesh.shape["dev"])
    return jax.shard_map(part, mesh=mesh, in_specs=in_specs, out_specs=out_specs, check_vma=False)
```

```python
import functools

import jax
import jax.numpy as jnp
from jax import lax
from jax.experimental import pallas as pl
from jax.experimental.layout import Layout, with_layout_constraint
from jax.experimental.pallas import tpu as pltpu
from jax.sharding import PartitionSpec as P

MESH = pl.DeviceIdType.MESH


def orthonormal(summed):
    gram_matrix = jnp.einsum("krs,krt->kst", summed, summed, precision=lax.Precision.HIGHEST)
    factor = jnp.linalg.cholesky(gram_matrix)
    solved = lax.linalg.triangular_solve(
        factor, summed, left_side=False, lower=True, transpose_a=True
    )
    return solved.astype(jnp.bfloat16)


def basis_kernel(groups, devs, part_ref, out_ref, pair, half, slots, work, gath,
                 pair_send, pair_recv, sum_send, sum_recv, all_send, all_recv,
                 share_send, share_recv):
    me_g, me_d = lax.axis_index("grp"), lax.axis_index("dev")
    blocks, rank, columns = part_ref.shape
    per_group = blocks // groups
    own = per_group // devs

    barrier = pltpu.get_barrier_semaphore()
    for step in range(1, groups):
        pl.semaphore_signal(barrier, inc=1, device_id=((me_g + step) % groups, me_d), device_id_type=MESH)

    @pl.loop(1, devs)
    def _(step):
        pl.semaphore_signal(barrier, inc=1, device_id=(me_g, (me_d + step) % devs), device_id_type=MESH)

    pl.semaphore_wait(barrier, groups - 1 + devs - 1)

    pair_copies = []
    for step in range(1, groups):
        peer = (me_g + step) % groups
        copy = pltpu.make_async_remote_copy(
            src_ref=part_ref.at[pl.ds(peer * per_group, per_group)],
            dst_ref=pair.at[step - 1],
            send_sem=pair_send.at[step - 1],
            recv_sem=pair_recv.at[step - 1],
            device_id=(peer, me_d),
            device_id_type=MESH,
        )
        copy.start()
        pair_copies.append(copy)
    for copy in pair_copies:
        copy.wait()

    @pl.loop(0, per_group)
    def _(b):
        value = part_ref[me_g * per_group + b]
        for step in range(1, groups):
            value += pair[step - 1, b]
        half[b] = value

    def to_owner(step):
        target = (me_d + step) % devs
        return pltpu.make_async_remote_copy(
            src_ref=half.at[pl.ds(target * own, own)],
            dst_ref=slots.at[step],
            send_sem=sum_send.at[step],
            recv_sem=sum_recv.at[step],
            device_id=(me_g, target),
            device_id_type=MESH,
        )

    @pl.loop(1, devs)
    def _(step):
        to_owner(step).start()

    work[...] = half[pl.ds(me_d * own, own)]

    @pl.loop(1, devs)
    def _(step):
        to_owner(step).wait()
        work[...] += slots[step]

    position = lax.broadcasted_iota(jnp.int32, (own, rank, columns), 1)

    @pl.loop(0, rank)
    def _(j):
        rows = work[...]
        row = work[:, pl.ds(j, 1), :]
        along = jnp.sum(rows * row, axis=2, keepdims=True)
        scale = lax.rsqrt(jnp.sum(row * row, axis=2, keepdims=True))
        unit = row * scale
        later = rows - (along * scale) * unit
        work[...] = jnp.where(position > j, later, jnp.where(position == j, jnp.broadcast_to(unit, rows.shape), rows))

    mine = me_g * per_group + me_d * own
    gath[pl.ds(mine, own)] = work[...].astype(gath.dtype)

    def to_all(step):
        return pltpu.make_async_remote_copy(
            src_ref=gath.at[pl.ds(mine, own)],
            dst_ref=gath.at[pl.ds(mine, own)],
            send_sem=all_send.at[step],
            recv_sem=all_recv.at[step],
            device_id=(me_g, (me_d + step) % devs),
            device_id_type=MESH,
        )

    @pl.loop(1, devs)
    def _(step):
        to_all(step).start()

    @pl.loop(1, devs)
    def _(step):
        to_all(step).wait()

    share_copies = []
    for step in range(1, groups):
        part = gath.at[pl.ds(me_g * per_group, per_group)]
        copy = pltpu.make_async_remote_copy(
            src_ref=part,
            dst_ref=part,
            send_sem=share_send.at[step - 1],
            recv_sem=share_recv.at[step - 1],
            device_id=((me_g + step) % groups, me_d),
            device_id_type=MESH,
        )
        copy.start()
        share_copies.append(copy)
    for copy in share_copies:
        copy.wait()

    @pl.loop(0, blocks)
    def _(b):
        out_ref[b] = gath[b]


def all_bases(groups, devs, partial):
    blocks, rank, columns = partial.shape
    per_group = blocks // groups
    own = per_group // devs
    dma = pltpu.SemaphoreType.DMA
    return pl.pallas_call(
        functools.partial(basis_kernel, groups, devs),
        out_shape=jax.ShapeDtypeStruct(partial.shape, jnp.bfloat16),
        in_specs=[pl.BlockSpec(memory_space=pltpu.VMEM)],
        out_specs=pl.BlockSpec(memory_space=pltpu.VMEM),
        scratch_shapes=[
            pltpu.VMEM((groups - 1, per_group, rank, columns), jnp.float32),
            pltpu.VMEM((per_group, rank, columns), jnp.float32),
            pltpu.VMEM((devs, own, rank, columns), jnp.float32),
            pltpu.VMEM((own, rank, columns), jnp.float32),
            pltpu.VMEM(partial.shape, jnp.bfloat16),
            dma((groups - 1,)),
            dma((groups - 1,)),
            dma((devs,)),
            dma((devs,)),
            dma((devs,)),
            dma((devs,)),
            dma((groups - 1,)),
            dma((groups - 1,)),
        ],
        compiler_params=pltpu.CompilerParams(
            collective_id=0, has_side_effects=True, vmem_limit_bytes=24 * 1024 * 1024
        ),
    )(partial)


def body(groups, devs, images, test_maps, counts):
    blocks, columns = images.shape[1:]
    radial = columns // 2
    position = lax.broadcasted_iota(jnp.int32, (blocks, columns), 1) % radial
    valid = position < counts[:, None]
    maps = jnp.where(valid[:, :, None], test_maps, jnp.zeros_like(test_maps))
    if groups > 1 and devs > 1 and blocks % (groups * devs) == 0:
        by_block = with_layout_constraint(images.transpose(1, 0, 2), Layout((0, 1, 2)))
        by_block = lax.optimization_barrier(by_block)
        sketch = jnp.einsum(
            "kir,krs->ksi", by_block, maps, preferred_element_type=jnp.float32
        ).astype(jnp.bfloat16)
        partial = jnp.einsum("kir,ksi->ksr", by_block, sketch, preferred_element_type=jnp.float32)
        partial = jnp.where(valid[:, None, :], partial, 0.0)
        basis_all = all_bases(groups, devs, partial)
        projected = jnp.einsum("kir,ksr->ksi", by_block, basis_all, preferred_element_type=jnp.float32)
        return projected.astype(jnp.bfloat16).transpose(2, 0, 1)
    else:
        sketch = jnp.einsum(
            "ikr,krs->iks", images, maps, preferred_element_type=jnp.float32
        ).astype(jnp.bfloat16)
        partial = jnp.einsum("ikr,iks->krs", images, sketch, preferred_element_type=jnp.float32)
        partial = jnp.where(valid[:, :, None], partial, 0.0)
        totals = lax.psum(partial, "grp")
        owned = lax.psum_scatter(totals, "dev", scatter_dimension=0, tiled=True)
        basis_all = lax.all_gather(orthonormal(owned), "dev", axis=0, tiled=True)
        projected = jnp.einsum("ikr,krs->iks", images, basis_all, preferred_element_type=jnp.float32)
    return projected.astype(jnp.bfloat16)


def solution(mesh):
    in_specs = (P(("grp", "dev"), None, None), P(), P())
    out_specs = P(("grp", "dev"), None, None)
    part = functools.partial(body, mesh.shape["grp"], mesh.shape["dev"])
    return jax.shard_map(part, mesh=mesh, in_specs=in_specs, out_specs=out_specs, check_vma=False)
```
